32 devices in a mesh: row: 8 (over z, x), slab: 4 (over y, core).
Axes of the slice: x: 2, y: 2, z: 4, core: 2. Of those that a mesh axis runs over, the one named last changes fastest.
Arguments:
- base_features: bfloat16 [64, 2048], P(None, ('row', 'slab')), may hold values from -0.8984375 to 0.8984375
- station_ids: int32 [2048], P(('row', 'slab')), may hold values from 0 to 511
- epoch_ids: int32 [2048], P(('row', 'slab')), may hold values from 0 to 511
- station_table: bfloat16 [64, 512], replicated, may hold values from -0.8984375 to 0.8984375
- epoch_table: bfloat16 [64, 512], replicated, may hold values from -0.8984375 to 0.8984375
- noise_var: float32 [2048], P(('row', 'slab')), may hold values from 0.05 to 1
- right_side: float32 [32, 2048], P(None, ('row', 'slab')), may hold values from -6 to 6
Outputs:
- solution: float32 [32, 2048], P(None, ('row', 'slab'))
- residual: float32 [32, 2048], P(None, ('row', 'slab'))
The draws below stay inside these ranges and needn't reach their ends.
All inputs are finite; a program needn't handle non-finite values.
Results may differ from the reference program's by a relative error of at most 0.012.
The reference program's roundings to bfloat16 on the way count: a program that leaves them out, or rounds other values in their place, can miss the bound.
Values may be sent and summed in bfloat16 or wider, within the bound.
A program may use at most 64 MiB of HBM per device.

```python
import math
import jax
import jax.numpy as jnp
from jax import lax

SAMPLES_DEV = 64
FEAT = 64
VECS = 32
STATIONS = 512
EPOCHS = 512
ITERS = 2
SAMPLES = 2048
N_SLAB = 4


def plant(entries, key, smallest, top_value):
    dims = entries.shape
    index_at = [jax.random.randint(jax.random.fold_in(key, axis), (), 0, dims[axis]) for axis in range(len(dims))]
    entries = entries.at[tuple(index_at)].set(smallest)
    longest = dims.index(max(dims))
    index_at[longest] = (index_at[longest] + 1) % dims[longest]
    return entries.at[tuple(index_at)].set(top_value)


def steps_of(rng, extent, shards, smallest, high):
    loudness = 1.0
    for axis_at, blocks in shards:
        heights = jax.random.uniform(jax.random.fold_in(jax.random.fold_in(rng, 6), axis_at), (blocks,), jnp.float32, smallest / len(shards), high / len(shards))
        loudness = loudness * jnp.repeat(jnp.exp(heights), extent[axis_at] // blocks).reshape((-1,) + (1,) * (len(extent) - 1 - axis_at))
    return loudness


def noise(stream_key, shape, spread, bound, cuts=(), kind=jnp.bfloat16):
    gain = steps_of(stream_key, shape, cuts, -0.22, 0.18) if cuts else 1.0
    result = jax.random.normal(stream_key, shape, jnp.float32) * spread * gain
    return jnp.minimum(jnp.maximum(result, -bound), bound).astype(kind)


def setup_inputs(seed: int = 0) -> dict:
    keys = jax.random.split(jax.random.key(seed), 8)
    base_features = noise(keys[0], (FEAT, SAMPLES), 0.15, 0.8984375, ((1, 32),))
    station_ids = plant(jax.random.randint(keys[1], (SAMPLES,), 0, STATIONS), jax.random.fold_in(keys[1], 1), 0, STATIONS - 1).astype(jnp.int32)
    epoch_ids = plant(jax.random.randint(keys[2], (SAMPLES,), 0, EPOCHS), jax.random.fold_in(keys[2], 1), 0, EPOCHS - 1).astype(jnp.int32)
    station_table = noise(keys[3], (FEAT, STATIONS), 0.15, 0.8984375)
    epoch_table = noise(keys[4], (FEAT, EPOCHS), 0.15, 0.8984375)
    noise_var = jnp.clip(jnp.exp(math.log(1.0) - 2.9957323 * jax.random.uniform(keys[5], (SAMPLES,), jnp.float32) ** steps_of(keys[5], (SAMPLES,), ((0, 32),), -0.2, 0.2)), 0.05, 1.0)
    right_side = noise(keys[6], (VECS, SAMPLES), 1.0, 6.0, ((1, 32),), jnp.float32)
    return dict(base_features=base_features, station_ids=station_ids, epoch_ids=epoch_ids, station_table=station_table, epoch_table=epoch_table, noise_var=noise_var, right_side=right_side)


def make_features(base_features, station_ids, epoch_ids, station_table, epoch_table):
    station_part = jnp.take(station_table.astype(jnp.float32), station_ids, axis=1)
    epoch_part = jnp.take(epoch_table.astype(jnp.float32), epoch_ids, axis=1)
    return (base_features.astype(jnp.float32) + station_part + epoch_part).astype(jnp.bfloat16)


def reference(base_features, station_ids, epoch_ids, station_table, epoch_table, noise_var, right_side):
    features = make_features(base_features, station_ids, epoch_ids, station_table, epoch_table)
    wide_feat = features.astype(jnp.float32)
    norms = jnp.sum(wide_feat * wide_feat, axis=0)
    block_rows = SAMPLES_DEV * N_SLAB
    count = SAMPLES // block_rows

    def operator(direction):
        rounded = direction.astype(jnp.bfloat16)
        rounded = lax.optimization_barrier(rounded).astype(jnp.float32)

        def one_block(start):
            rows_feat = lax.dynamic_slice_in_dim(wide_feat, start, block_rows, 1)
            rows_norm = lax.dynamic_slice_in_dim(norms, start, block_rows, 0)
            cross_term = jnp.dot(wide_feat.T, rows_feat, precision=lax.Precision.HIGHEST,
                                 preferred_element_type=jnp.float32)
            distance = jnp.maximum((norms[:, None] + rows_norm[None, :]) - 2.0 * cross_term, 0.0)
            kernel_tile = jnp.exp(-0.5 * distance).astype(jnp.bfloat16)
            kernel_tile = lax.optimization_barrier(kernel_tile).astype(jnp.float32)
            return jnp.dot(rounded, kernel_tile, precision=lax.Precision.HIGHEST,
                           preferred_element_type=jnp.float32)

        starts = (jnp.arange(count) * block_rows).astype(jnp.int32)
        blocks = lax.map(one_block, starts)
        product = jnp.transpose(blocks, (1, 0, 2)).reshape(VECS, SAMPLES)
        return product + noise_var[None, :] * direction

    solution = jnp.zeros_like(right_side)
    residual = right_side
    direction = right_side
    res_norm = jnp.sum(residual * residual, axis=1)
    for iteration in range(ITERS):
        image = operator(direction)
        step_size = res_norm / jnp.sum(direction * image, axis=1)
        solution = solution + step_size[:, None] * direction
        residual = residual - step_size[:, None] * image
        if iteration + 1 < ITERS:
            new_norm = jnp.sum(residual * residual, axis=1)
            direction = residual + (new_norm / res_norm)[:, None] * direction
            res_norm = new_norm
    return solution, residual
```

```python
import functools

import jax
import jax.numpy as jnp
from jax import lax
from jax.experimental import pallas as pl
from jax.experimental.pallas import tpu as pltpu
from jax.sharding import PartitionSpec as P

ITERS = 2


def lookup(table, indices):
    positions = lax.broadcasted_iota(jnp.int32, (table.shape[1], indices.shape[0]), 0)
    one_hot = (positions == indices[None, :]).astype(jnp.bfloat16)
    return jnp.dot(table, one_hot, preferred_element_type=jnp.float32)


def column_norms(piece):
    wide_piece = piece.astype(jnp.float32)
    return jnp.sum(wide_piece * wide_piece, axis=0)


def tile_term(col_feat, col_dir, rows_feat, rows_norm):
    cross_term = lax.dot_general(
        col_feat, rows_feat, (((0,), (0,)), ((), ())), preferred_element_type=jnp.float32
    )
    col_norm = column_norms(col_feat)
    distance = jnp.maximum(col_norm[:, None] + rows_norm[None, :] - 2.0 * cross_term, 0.0)
    kernel_tile = jnp.exp(-0.5 * distance).astype(jnp.bfloat16)
    return jnp.dot(col_dir, kernel_tile, preferred_element_type=jnp.float32)


def global_dot(left, right):
    return lax.psum(jnp.sum(left * right, axis=1), ("row", "slab"))


def per_device(
    base_features, station_ids, epoch_ids, station_table, epoch_table, noise_var, right_side
):
    own_feat = (
        base_features.astype(jnp.float32)
        + lookup(station_table, station_ids)
        + lookup(epoch_table, epoch_ids)
    ).astype(jnp.bfloat16)
    rows_feat = lax.all_gather(own_feat, "slab", axis=1, tiled=True)
    rows_norm = column_norms(rows_feat)
    solution = jnp.zeros_like(right_side)
    residual = right_side
    direction = right_side
    res_norm = global_dot(residual, residual)
    for iteration in range(ITERS):
        rounded = direction.astype(jnp.bfloat16)
        partial_value = tile_term(
            lax.all_gather(own_feat, "row", axis=1, tiled=True),
            lax.all_gather(rounded, "row", axis=1, tiled=True),
            rows_feat,
            rows_norm,
        )
        product = lax.psum_scatter(partial_value, "slab", scatter_dimension=1, tiled=True)
        image = product + noise_var[None, :] * direction
        curvature = global_dot(direction, image)
        step_size = res_norm / curvature
        solution = solution + step_size[:, None] * direction
        residual = residual - step_size[:, None] * image
        if iteration + 1 < ITERS:
            new_norm = global_dot(residual, residual)
            direction = residual + (new_norm / res_norm)[:, None] * direction
            res_norm = new_norm
    return (solution, residual)


MESH = pl.DeviceIdType.MESH
NT = (((1,), (1,)), ((), ()))
HALF = 64


def dot_nt(left, right, precision=None):
    return lax.dot_general(left, right, NT, precision=precision, preferred_element_type=jnp.float32)


def lane_mask(rows):
    return lax.broadcasted_iota(jnp.int32, (rows, 128), 1) < HALF


def swap(value):
    return pltpu.roll(value, HALF, 1)


def fold(wide, odd):
    half = wide.shape[0] // 2
    top, bottom = wide[:half], wide[half:]
    if odd:
        return jnp.where(lane_mask(half), swap(top), bottom)
    return jnp.where(lane_mask(half), top, swap(bottom))


def unfold_pair(first, second):
    mask = lane_mask(first.shape[0])
    top = jnp.where(mask, first, swap(second))
    bottom = jnp.where(mask, swap(first), second)
    return jnp.concatenate([top, bottom], axis=0)


def unfold_all(blocks):
    pairs = [unfold_pair(blocks[k], blocks[k + 1]) for k in range(0, len(blocks), 2)]
    return jnp.concatenate(pairs, axis=1)


def split_rows(folded):
    mask = lane_mask(folded.shape[0])
    zero = jnp.zeros_like(folded)
    return jnp.concatenate([jnp.where(mask, folded, zero), jnp.where(mask, zero, folded)], axis=0)


def solve_kernel(
    n_row, n_slab,
    base_hbm, sid_hbm, eid_hbm, station_hbm, epoch_hbm, noise_hbm, right_hbm,
    sol_out, res_out,
    base_v, sid_v, eid_v, station_v, epoch_v, noise_v, right_v,
    col_v, row_v, kernel_v, part1_v, sum1_v, qcol_v, qrow_v, part2_v, sum2_v, mom_v, mom_in,
    load_sem, s_g1, r_g1, s_g1r, r_g1r, s_rs1, r_rs1, s_g2, r_g2, s_g2r, r_g2r, s_rs2, r_rs2, s_ar, r_ar,
):
    row, slab = lax.axis_index("row"), lax.axis_index("slab")
    feat, samples = base_hbm.shape
    vecs = right_hbm.shape[0]
    n_dev = n_row * n_slab

    def row_peer(k):
        return (lax.rem(row + k, n_row), slab)

    def slab_peer(k):
        return (row, lax.rem(slab + k, n_slab))

    def remote(src, dst, send, recv, peer):
        copy = pltpu.make_async_remote_copy(
            src_ref=src, dst_ref=dst, send_sem=send, recv_sem=recv, device_id=peer, device_id_type=MESH
        )
        copy.start()
        return copy

    barrier = pltpu.get_barrier_semaphore()
    for k in range(1, n_row):
        pl.semaphore_signal(barrier, inc=1, device_id=row_peer(k), device_id_type=MESH)
    for k in range(1, n_slab):
        pl.semaphore_signal(barrier, inc=1, device_id=slab_peer(k), device_id_type=MESH)

    loads = []
    for k, (src, dst) in enumerate((
        (sid_hbm, sid_v), (eid_hbm, eid_v), (station_hbm, station_v), (epoch_hbm, epoch_v),
        (base_hbm, base_v), (right_hbm, right_v), (noise_hbm, noise_v),
    )):
        copy = pltpu.make_async_copy(src, dst, load_sem.at[k])
        copy.start()
        loads.append(copy)
    for copy in loads:
        copy.wait()

    def gather(table, ids):
        positions = lax.broadcasted_iota(jnp.int32, (table.shape[1], samples), 0)
        one_hot = jnp.where(positions == ids, 1.0, 0.0).astype(jnp.bfloat16)
        return jnp.dot(table, one_hot, preferred_element_type=jnp.float32)

    right = right_v[...]
    own = (
        base_v[...].astype(jnp.float32)
        + gather(station_v[...], sid_v[...])
        + gather(epoch_v[...], eid_v[...])
    ).astype(jnp.bfloat16).astype(jnp.float32)
    norm = -0.5 * jnp.sum(own * own, axis=0, keepdims=True)
    high = norm.astype(jnp.bfloat16).astype(jnp.float32)
    middle = (norm - high).astype(jnp.bfloat16).astype(jnp.float32)
    low = norm - high - middle
    at = lax.broadcasted_iota(jnp.int32, (8, samples), 0)
    one, nil = jnp.ones((8, samples), jnp.float32), jnp.zeros((8, samples), jnp.float32)
    col_norm = jnp.where(at == 0, high, jnp.where(at == 1, middle, jnp.where(at == 2, low, jnp.where(at < 6, one, nil))))
    row_norm = jnp.where(at < 3, one, jnp.where(at == 3, high, jnp.where(at == 4, middle, jnp.where(at == 5, low, nil))))
    rest = jnp.zeros((128 - feat - vecs - 8, samples), jnp.float32)
    stacked = jnp.concatenate(
        [own, right, col_norm, rest, own, jnp.zeros((vecs, samples), jnp.float32), row_norm, rest], axis=0
    ).astype(jnp.bfloat16)
    eye_r = lax.broadcasted_iota(jnp.int32, (samples, samples), 0)
    eye_c = lax.broadcasted_iota(jnp.int32, (samples, samples), 1)
    eye = jnp.where(eye_r == eye_c, 1.0, 0.0).astype(jnp.bfloat16)
    packs = dot_nt(eye, stacked).astype(jnp.bfloat16)
    col_v[0] = packs[:, :128]
    row_v[0] = packs[:, 128:]

    pl.semaphore_wait(barrier, n_row + n_slab - 2)
    g1 = [remote(col_v.at[0], col_v.at[k], s_g1.at[k], r_g1.at[k], row_peer(k)) for k in range(1, n_row)]
    g1 += [remote(row_v.at[0], row_v.at[k], s_g1r.at[k], r_g1r.at[k], slab_peer(k)) for k in range(1, n_slab)]

    half = vecs // 2
    right_f = jnp.concatenate([right[:half], right[half:]], axis=1)
    noise_f = jnp.concatenate([noise_v[...], noise_v[...]], axis=1)
    pick_r = lax.broadcasted_iota(jnp.int32, (vecs, 128), 0)
    pick_c = lax.broadcasted_iota(jnp.int32, (vecs, 128), 1)
    pick = jnp.where(pick_c == pick_r + feat, 1.0, 0.0).astype(jnp.bfloat16)

    for copy in g1:
        copy.wait_recv()

    cols = col_v[...].reshape(n_row * samples, 128)
    rows = row_v[...].reshape(n_slab * samples, 128)
    logits = dot_nt(cols, rows)
    directions = dot_nt(pick, cols).astype(jnp.bfloat16)
    kernel_v[...] = jnp.exp(jnp.minimum(logits, 0.0)).astype(jnp.bfloat16)
    tile = kernel_v[...]
    part = jnp.dot(directions, tile, preferred_element_type=jnp.float32)

    def reduce_start(part, out_v, in_v, send, recv):
        copies = []
        for k in range(n_slab - 1, -1, -1):
            start = 128 * (k // 2)
            out_v[k] = fold(part[:, start:start + 128], k % 2)
            if k:
                copies.append(remote(out_v.at[k], in_v.at[k], send.at[k], recv.at[k], slab_peer(n_slab - k)))
        return copies

    def reduce_end(copies, out_v, in_v):
        for copy in copies:
            copy.wait_recv()
        total = out_v[0]
        for k in range(1, n_slab):
            total = total + in_v[k]
        return total

    rs1 = reduce_start(part, part1_v, sum1_v, s_rs1, r_rs1)
    image = reduce_end(rs1, part1_v, sum1_v) + noise_f * right_f

    rounded = image.astype(jnp.bfloat16)
    qcol_v[0] = rounded
    g2 = [remote(qcol_v.at[0], qcol_v.at[k], s_g2.at[k], r_g2.at[k], row_peer(k)) for k in range(1, n_row)]
    g2 += [remote(qcol_v.at[0], qrow_v.at[k], s_g2r.at[k], r_g2r.at[k], slab_peer(k)) for k in range(1, n_slab)]
    qrow_v[0] = rounded

    early = jnp.concatenate(
        [split_rows(right_f * right_f), split_rows(right_f * image), split_rows(image * image),
         split_rows(noise_f * image * image)], axis=0
    )
    moments = dot_nt(jnp.ones((8, 128), jnp.float32), early, lax.Precision.HIGHEST)

    for copy in g2:
        copy.wait_recv()
    images = unfold_all([qcol_v[k].astype(jnp.float32) for k in range(n_row)]).astype(jnp.bfloat16)
    part = jnp.dot(images, tile, preferred_element_type=jnp.float32)
    rs2 = reduce_start(part, part2_v, sum2_v, s_rs2, r_rs2)
    own_rows = unfold_all([qrow_v[k].astype(jnp.float32) for k in range(n_slab)])
    late = jnp.concatenate([jnp.zeros((3 * vecs, part.shape[1]), jnp.float32), own_rows * part], axis=0)
    moments = moments + dot_nt(jnp.ones((8, part.shape[1]), jnp.float32), late, lax.Precision.HIGHEST)
    mom_v[...] = moments[:1]

    me = row * n_slab + slab
    ar = []
    for k in range(1, n_dev):
        other = lax.rem(me + k, n_dev)
        peer = (other // n_slab, lax.rem(other, n_slab))
        ar.append(remote(mom_v, mom_in.at[k], s_ar.at[k], r_ar.at[k], peer))
    second = reduce_end(rs2, part2_v, sum2_v) + noise_f * image
    mask = lane_mask(half)
    image_n = jnp.concatenate([image, swap(image)], axis=0)[:, :samples]
    second_n = jnp.concatenate([second, swap(second)], axis=0)[:, :samples]

    for copy in ar:
        copy.wait_recv()
    total = mom_v[...]
    for k in range(1, n_dev):
        total = total + mom_in[k]
    total = jnp.broadcast_to(total, (8, 128))
    bb = total
    bq, qq, qs = (pltpu.roll(total, 128 - vecs * k, 1) for k in (1, 2, 3))
    alpha = bb / bq
    fresh = bb - 2.0 * alpha * bq + alpha * alpha * qq
    grow = 1.0 + fresh / bb
    curvature = grow * grow * bq - 2.0 * alpha * grow * qq + alpha * alpha * qs
    step = fresh / curvature
    first_c = alpha + step * grow
    second_c = step * alpha

    def column(coefficients):
        spread = jnp.where(pick_r == pick_c, coefficients[:1], 0.0)
        return jnp.sum(spread, axis=1, keepdims=True)

    first_c, second_c = column(first_c), column(second_c)
    sol_out[...] = first_c * right - second_c * image_n
    res_out[...] = right - first_c * image_n + second_c * second_n

    for copy in g1 + rs1 + g2 + rs2 + ar:
        copy.wait_send()


def per_device_kernel(
    n_row, n_slab, base_features, station_ids, epoch_ids, station_table, epoch_table, noise_var, right_side
):
    feat, samples = base_features.shape
    vecs = right_side.shape[0]
    n_dev = n_row * n_slab
    bf16, f32 = jnp.bfloat16, jnp.float32
    dma = pltpu.SemaphoreType.DMA
    half = vecs // 2
    operands = (
        base_features, station_ids.reshape(1, samples), epoch_ids.reshape(1, samples),
        station_table, epoch_table, noise_var.reshape(1, samples), right_side,
    )
    shape = jax.ShapeDtypeStruct((vecs, samples), f32)
    return pl.pallas_call(
        functools.partial(solve_kernel, n_row, n_slab),
        out_shape=(shape, shape),
        in_specs=[pl.BlockSpec(memory_space=pl.ANY)] * 7,
        out_specs=(pl.BlockSpec(memory_space=pltpu.VMEM),) * 2,
        scratch_shapes=[pltpu.VMEM(x.shape, x.dtype) for x in operands] + [
            pltpu.VMEM((n_row, samples, 128), bf16),
            pltpu.VMEM((n_slab, samples, 128), bf16),
            pltpu.VMEM((n_row * samples, n_slab * samples), bf16),
            pltpu.VMEM((n_slab, half, 128), f32),
            pltpu.VMEM((n_slab, half, 128), f32),
            pltpu.VMEM((n_row, half, 128), bf16),
            pltpu.VMEM((n_slab, half, 128), bf16),
            pltpu.VMEM((n_slab, half, 128), f32),
            pltpu.VMEM((n_slab, half, 128), f32),
            pltpu.VMEM((1, 128), f32),
            pltpu.VMEM((n_dev, 1, 128), f32),
            dma((7,)),
            dma((n_row,)), dma((n_row,)), dma((n_slab,)), dma((n_slab,)),
            dma((n_slab,)), dma((n_slab,)),
            dma((n_row,)), dma((n_row,)), dma((n_slab,)), dma((n_slab,)),
            dma((n_slab,)), dma((n_slab,)),
            dma((n_dev,)), dma((n_dev,)),
        ],
        compiler_params=pltpu.CompilerParams(
            collective_id=0, has_side_effects=True, vmem_limit_bytes=16 * 1024 * 1024
        ),
    )(*operands)


def solution(mesh):
    in_specs = (
        P(None, ("row", "slab")),
        P(("row", "slab")),
        P(("row", "slab")),
        P(),
        P(),
        P(("row", "slab")),
        P(None, ("row", "slab")),
    )
    out_specs = (P(None, ("row", "slab")), P(None, ("row", "slab")))
    n_row, n_slab = mesh.shape["row"], mesh.shape["slab"]
    body = per_device
    if n_row * n_slab <= 64:
        body = functools.partial(per_device_kernel, n_row, n_slab)
    return jax.shard_map(
        body, mesh=mesh, in_specs=in_specs, out_specs=out_specs, check_vma=False
    )
```

```python
import functools

import jax
import jax.numpy as jnp
from jax import lax
from jax.experimental import pallas as pl
from jax.experimental.pallas import tpu as pltpu
from jax.sharding import PartitionSpec as P

ITERS = 2


def lookup(table, indices):
    positions = lax.broadcasted_iota(jnp.int32, (table.shape[1], indices.shape[0]), 0)
    one_hot = (positions == indices[None, :]).astype(jnp.bfloat16)
    return jnp.dot(table, one_hot, preferred_element_type=jnp.float32)


def column_norms(piece):
    wide_piece = piece.astype(jnp.float32)
    return jnp.sum(wide_piece * wide_piece, axis=0)


def tile_term(col_feat, col_dir, rows_feat, rows_norm):
    cross_term = lax.dot_general(
        col_feat, rows_feat, (((0,), (0,)), ((), ())), preferred_element_type=jnp.float32
    )
    col_norm = column_norms(col_feat)
    distance = jnp.maximum(col_norm[:, None] + rows_norm[None, :] - 2.0 * cross_term, 0.0)
    kernel_tile = jnp.exp(-0.5 * distance).astype(jnp.bfloat16)
    return jnp.dot(col_dir, kernel_tile, preferred_element_type=jnp.float32)


def global_dot(left, right):
    return lax.psum(jnp.sum(left * right, axis=1), ("row", "slab"))


def per_device(
    base_features, station_ids, epoch_ids, station_table, epoch_table, noise_var, right_side
):
    own_feat = (
        base_features.astype(jnp.float32)
        + lookup(station_table, station_ids)
        + lookup(epoch_table, epoch_ids)
    ).astype(jnp.bfloat16)
    rows_feat = lax.all_gather(own_feat, "slab", axis=1, tiled=True)
    rows_norm = column_norms(rows_feat)
    solution = jnp.zeros_like(right_side)
    residual = right_side
    direction = right_side
    res_norm = global_dot(residual, residual)
    for iteration in range(ITERS):
        rounded = direction.astype(jnp.bfloat16)
        partial_value = tile_term(
            lax.all_gather(own_feat, "row", axis=1, tiled=True),
            lax.all_gather(rounded, "row", axis=1, tiled=True),
            rows_feat,
            rows_norm,
        )
        product = lax.psum_scatter(partial_value, "slab", scatter_dimension=1, tiled=True)
        image = product + noise_var[None, :] * direction
        curvature = global_dot(direction, image)
        step_size = res_norm / curvature
        solution = solution + step_size[:, None] * direction
        residual = residual - step_size[:, None] * image
        if iteration + 1 < ITERS:
            new_norm = global_dot(residual, residual)
            direction = residual + (new_norm / res_norm)[:, None] * direction
            res_norm = new_norm
    return (solution, residual)


MESH = pl.DeviceIdType.MESH
NT = (((1,), (1,)), ((), ()))
HALF = 64


def dot_nt(left, right, precision=None):
    return lax.dot_general(left, right, NT, precision=precision, preferred_element_type=jnp.float32)


def lane_mask(rows):
    return lax.broadcasted_iota(jnp.int32, (rows, 128), 1) < HALF


def swap(value):
    return pltpu.roll(value, HALF, 1)


def fold(wide, odd):
    half = wide.shape[0] // 2
    top, bottom = wide[:half], wide[half:]
    if odd:
        return jnp.where(lane_mask(half), swap(top), bottom)
    return jnp.where(lane_mask(half), top, swap(bottom))


def unfold_pair(first, second):
    mask = lane_mask(first.shape[0])
    top = jnp.where(mask, first, swap(second))
    bottom = jnp.where(mask, swap(first), second)
    return jnp.concatenate([top, bottom], axis=0)


def unfold_all(blocks):
    pairs = [unfold_pair(blocks[k], blocks[k + 1]) for k in range(0, len(blocks), 2)]
    return jnp.concatenate(pairs, axis=1)


def split_rows(folded):
    mask = lane_mask(folded.shape[0])
    zero = jnp.zeros_like(folded)
    return jnp.concatenate([jnp.where(mask, folded, zero), jnp.where(mask, zero, folded)], axis=0)


def solve_kernel(
    n_row, n_slab,
    base_hbm, sid_hbm, eid_hbm, station_hbm, epoch_hbm, noise_hbm, right_hbm,
    both_out,
    base_v, sid_v, eid_v, station_v, epoch_v, noise_v, right_v,
    col_v, row_v, kernel_v, part1_v, sum1_v, qcol_v, qrow_v, part2_v, sum2_v, mom_v, mom_in,
    load_sem, s_g1, r_g1, s_g1r, r_g1r, s_rs1, r_rs1, s_g2, r_g2, s_g2r, r_g2r, s_rs2, r_rs2, s_ar, r_ar,
):
    row, slab = lax.axis_index("row"), lax.axis_index("slab")
    feat, samples = base_hbm.shape
    vecs = right_hbm.shape[0]
    n_dev = n_row * n_slab

    def row_peer(k):
        return (lax.rem(row + k, n_row), slab)

    def slab_peer(k):
        return (row, lax.rem(slab + k, n_slab))

    def remote(src, dst, send, recv, peer):
        copy = pltpu.make_async_remote_copy(
            src_ref=src, dst_ref=dst, send_sem=send, recv_sem=recv, device_id=peer, device_id_type=MESH
        )
        copy.start()
        return copy

    barrier = pltpu.get_barrier_semaphore()
    for k in range(1, n_row):
        pl.semaphore_signal(barrier, inc=1, device_id=row_peer(k), device_id_type=MESH)
    for k in range(1, n_slab):
        pl.semaphore_signal(barrier, inc=1, device_id=slab_peer(k), device_id_type=MESH)

    loads = []
    for k, (src, dst) in enumerate((
        (sid_hbm, sid_v), (eid_hbm, eid_v), (station_hbm, station_v), (epoch_hbm, epoch_v),
        (base_hbm, base_v), (right_hbm, right_v), (noise_hbm, noise_v),
    )):
        copy = pltpu.make_async_copy(src, dst, load_sem.at[k])
        copy.start()
        loads.append(copy)
    for copy in loads:
        copy.wait()

    def gather(table, ids):
        positions = lax.broadcasted_iota(jnp.int32, (table.shape[1], samples), 0)
        one_hot = jnp.where(positions == ids, 1.0, 0.0).astype(jnp.bfloat16)
        return jnp.dot(table, one_hot, preferred_element_type=jnp.float32)

    right = right_v[...]
    own = (
        base_v[...].astype(jnp.float32)
        + gather(station_v[...], sid_v[...])
        + gather(epoch_v[...], eid_v[...])
    ).astype(jnp.bfloat16).astype(jnp.float32)
    norm = -0.5 * jnp.sum(own * own, axis=0, keepdims=True)
    high = norm.astype(jnp.bfloat16).astype(jnp.float32)
    middle = (norm - high).astype(jnp.bfloat16).astype(jnp.float32)
    low = norm - high - middle
    at = lax.broadcasted_iota(jnp.int32, (8, samples), 0)
    one, nil = jnp.ones((8, samples), jnp.float32), jnp.zeros((8, samples), jnp.float32)
    col_norm = jnp.where(at == 0, high, jnp.where(at == 1, middle, jnp.where(at == 2, low, jnp.where(at < 6, one, nil))))
    row_norm = jnp.where(at < 3, one, jnp.where(at == 3, high, jnp.where(at == 4, middle, jnp.where(at == 5, low, nil))))
    rest = jnp.zeros((128 - feat - vecs - 8, samples), jnp.float32)
    stacked = jnp.concatenate(
        [own, right, col_norm, rest, own, jnp.zeros((vecs, samples), jnp.float32), row_norm, rest], axis=0
    ).astype(jnp.bfloat16)
    eye_r = lax.broadcasted_iota(jnp.int32, (samples, samples), 0)
    eye_c = lax.broadcasted_iota(jnp.int32, (samples, samples), 1)
    eye = jnp.where(eye_r == eye_c, 1.0, 0.0).astype(jnp.bfloat16)
    packs = dot_nt(eye, stacked).astype(jnp.bfloat16)
    col_v[0] = packs[:, :128]
    row_v[0] = packs[:, 128:]

    pl.semaphore_wait(barrier, n_row + n_slab - 2)
    g1 = [remote(col_v.at[0], col_v.at[k], s_g1.at[k], r_g1.at[k], row_peer(k)) for k in range(1, n_row)]
    g1 += [remote(row_v.at[0], row_v.at[k], s_g1r.at[k], r_g1r.at[k], slab_peer(k)) for k in range(1, n_slab)]

    half = vecs // 2
    right_f = jnp.concatenate([right[:half], right[half:]], axis=1)
    noise_f = jnp.concatenate([noise_v[...], noise_v[...]], axis=1)
    pick_r = lax.broadcasted_iota(jnp.int32, (vecs, 128), 0)
    pick_c = lax.broadcasted_iota(jnp.int32, (vecs, 128), 1)
    pick = jnp.where(pick_c == pick_r + feat, 1.0, 0.0).astype(jnp.bfloat16)

    for copy in g1:
        copy.wait_recv()

    cols = col_v[...].reshape(n_row * samples, 128)
    rows = row_v[...].reshape(n_slab * samples, 128)
    logits = dot_nt(cols, rows)
    directions = dot_nt(pick, cols).astype(jnp.bfloat16)
    kernel_v[...] = jnp.exp(jnp.minimum(logits, 0.0)).astype(jnp.bfloat16)
    tile = kernel_v[...]
    part = jnp.dot(directions, tile, preferred_element_type=jnp.float32)

    def reduce_start(part, out_v, in_v, send, recv):
        copies = []
        for k in range(n_slab - 1, -1, -1):
            start = 128 * (k // 2)
            out_v[k] = fold(part[:, start:start + 128], k % 2)
            if k:
                copies.append(remote(out_v.at[k], in_v.at[k], send.at[k], recv.at[k], slab_peer(n_slab - k)))
        return copies

    def reduce_end(copies, out_v, in_v):
        for copy in copies:
            copy.wait_recv()
        total = out_v[0]
        for k in range(1, n_slab):
            total = total + in_v[k]
        return total

    rs1 = reduce_start(part, part1_v, sum1_v, s_rs1, r_rs1)
    image = reduce_end(rs1, part1_v, sum1_v) + noise_f * right_f

    rounded = image.astype(jnp.bfloat16)
    qcol_v[0] = rounded
    g2 = [remote(qcol_v.at[0], qcol_v.at[k], s_g2.at[k], r_g2.at[k], row_peer(k)) for k in range(1, n_row)]
    g2 += [remote(qcol_v.at[0], qrow_v.at[k], s_g2r.at[k], r_g2r.at[k], slab_peer(k)) for k in range(1, n_slab)]
    qrow_v[0] = rounded

    early = jnp.concatenate(
        [split_rows(right_f * right_f), split_rows(right_f * image), split_rows(image * image),
         split_rows(noise_f * image * image)], axis=0
    )
    moments = dot_nt(jnp.ones((8, 128), jnp.float32), early, lax.Precision.HIGHEST)

    for copy in g2:
        copy.wait_recv()
    images = unfold_all([qcol_v[k].astype(jnp.float32) for k in range(n_row)]).astype(jnp.bfloat16)
    part = jnp.dot(images, tile, preferred_element_type=jnp.float32)
    rs2 = reduce_start(part, part2_v, sum2_v, s_rs2, r_rs2)
    own_rows = unfold_all([qrow_v[k].astype(jnp.float32) for k in range(n_slab)])
    late = jnp.concatenate([jnp.zeros((3 * vecs, part.shape[1]), jnp.float32), own_rows * part], axis=0)
    ones = jnp.ones((8, part.shape[1]), jnp.bfloat16)
    late_high = late.astype(jnp.bfloat16)
    late_low = (late - late_high.astype(jnp.float32)).astype(jnp.bfloat16)
    moments = moments + (dot_nt(ones, late_high) + dot_nt(ones, late_low))
    mom_v[...] = moments[:1]

    me = row * n_slab + slab
    ar = []
    for k in range(1, n_dev):
        other = lax.rem(me + k, n_dev)
        peer = (other // n_slab, lax.rem(other, n_slab))
        ar.append(remote(mom_v, mom_in.at[k], s_ar.at[k], r_ar.at[k], peer))
    second = reduce_end(rs2, part2_v, sum2_v) + noise_f * image
    mask = lane_mask(half)
    image_n = jnp.concatenate([image, swap(image)], axis=0)[:, :samples]
    second_n = jnp.concatenate([second, swap(second)], axis=0)[:, :samples]

    for copy in ar:
        copy.wait_recv()
    total = mom_v[...]
    for k in range(1, n_dev):
        total = total + mom_in[k]
    total = jnp.broadcast_to(total, (8, 128))
    bb = total
    bq, qq, qs = (pltpu.roll(total, 128 - vecs * k, 1) for k in (1, 2, 3))
    alpha = bb / bq
    fresh = bb - 2.0 * alpha * bq + alpha * alpha * qq
    grow = 1.0 + fresh / bb
    curvature = grow * grow * bq - 2.0 * alpha * grow * qq + alpha * alpha * qs
    step = fresh / curvature
    first_c = alpha + step * grow
    second_c = step * alpha

    def column(coefficients):
        spread = jnp.where(pick_r == pick_c, coefficients[:1], 0.0)
        return jnp.sum(spread, axis=1, keepdims=True)

    first_c, second_c = column(first_c), column(second_c)
    both_out[0] = first_c * right - second_c * image_n
    both_out[1] = right - first_c * image_n + second_c * second_n

    for copy in g1 + rs1 + g2 + rs2 + ar:
        copy.wait_send()


def per_device_kernel(
    n_row, n_slab, base_features, station_ids, epoch_ids, station_table, epoch_table, noise_var, right_side
):
    feat, samples = base_features.shape
    vecs = right_side.shape[0]
    n_dev = n_row * n_slab
    bf16, f32 = jnp.bfloat16, jnp.float32
    dma = pltpu.SemaphoreType.DMA
    half = vecs // 2
    operands = (
        base_features, station_ids.reshape(1, samples), epoch_ids.reshape(1, samples),
        station_table, epoch_table, noise_var.reshape(1, samples), right_side,
    )
    shape = jax.ShapeDtypeStruct((2, vecs, samples), f32)
    both = pl.pallas_call(
        functools.partial(solve_kernel, n_row, n_slab),
        out_shape=shape,
        in_specs=[pl.BlockSpec(memory_space=pl.ANY)] * 7,
        out_specs=pl.BlockSpec(memory_space=pltpu.VMEM),
        scratch_shapes=[pltpu.VMEM(x.shape, x.dtype) for x in operands] + [
            pltpu.VMEM((n_row, samples, 128), bf16),
            pltpu.VMEM((n_slab, samples, 128), bf16),
            pltpu.VMEM((n_row * samples, n_slab * samples), bf16),
            pltpu.VMEM((n_slab, half, 128), f32),
            pltpu.VMEM((n_slab, half, 128), f32),
            pltpu.VMEM((n_row, half, 128), bf16),
            pltpu.VMEM((n_slab, half, 128), bf16),
            pltpu.VMEM((n_slab, half, 128), f32),
            pltpu.VMEM((n_slab, half, 128), f32),
            pltpu.VMEM((1, 128), f32),
            pltpu.VMEM((n_dev, 1, 128), f32),
            dma((7,)),
            dma((n_row,)), dma((n_row,)), dma((n_slab,)), dma((n_slab,)),
            dma((n_slab,)), dma((n_slab,)),
            dma((n_row,)), dma((n_row,)), dma((n_slab,)), dma((n_slab,)),
            dma((n_slab,)), dma((n_slab,)),
            dma((n_dev,)), dma((n_dev,)),
        ],
        compiler_params=pltpu.CompilerParams(
            collective_id=0, has_side_effects=True, vmem_limit_bytes=60 * 1024 * 1024
        ),
    )(*operands)
    return both[0], both[1]


def solution(mesh):
    in_specs = (
        P(None, ("row", "slab")),
        P(("row", "slab")),
        P(("row", "slab")),
        P(),
        P(),
        P(("row", "slab")),
        P(None, ("row", "slab")),
    )
    out_specs = (P(None, ("row", "slab")), P(None, ("row", "slab")))
    n_row, n_slab = mesh.shape["row"], mesh.shape["slab"]
    body = per_device
    if n_row * n_slab <= 64:
        body = functools.partial(per_device_kernel, n_row, n_slab)
    return jax.shard_map(
        body, mesh=mesh, in_specs=in_specs, out_specs=out_specs, check_vma=False
    )
```

```python
import functools

import jax
import jax.numpy as jnp
from jax import lax
from jax.experimental import pallas as pl
from jax.experimental.pallas import tpu as pltpu
from jax.sharding import PartitionSpec as P

ITERS = 2


def lookup(table, indices):
    positions = lax.broadcasted_iota(jnp.int32, (table.shape[1], indices.shape[0]), 0)
    one_hot = (positions == indices[None, :]).astype(jnp.bfloat16)
    return jnp.dot(table, one_hot, preferred_element_type=jnp.float32)


def column_norms(piece):
    wide_piece = piece.astype(jnp.float32)
    return jnp.sum(wide_piece * wide_piece, axis=0)


def tile_term(col_feat, col_dir, rows_feat, rows_norm):
    cross_term = lax.dot_general(
        col_feat, rows_feat, (((0,), (0,)), ((), ())), preferred_element_type=jnp.float32
    )
    col_norm = column_norms(col_feat)
    distance = jnp.maximum(col_norm[:, None] + rows_norm[None, :] - 2.0 * cross_term, 0.0)
    kernel_tile = jnp.exp(-0.5 * distance).astype(jnp.bfloat16)
    return jnp.dot(col_dir, kernel_tile, preferred_element_type=jnp.float32)


def global_dot(left, right):
    return lax.psum(jnp.sum(left * right, axis=1), ("row", "slab"))


def per_device(
    base_features, station_ids, epoch_ids, station_table, epoch_table, noise_var, right_side
):
    own_feat = (
        base_features.astype(jnp.float32)
        + lookup(station_table, station_ids)
        + lookup(epoch_table, epoch_ids)
    ).astype(jnp.bfloat16)
    rows_feat = lax.all_gather(own_feat, "slab", axis=1, tiled=True)
    rows_norm = column_norms(rows_feat)
    solution = jnp.zeros_like(right_side)
    residual = right_side
    direction = right_side
    res_norm = global_dot(residual, residual)
    for iteration in range(ITERS):
        rounded = direction.astype(jnp.bfloat16)
        partial_value = tile_term(
            lax.all_gather(own_feat, "row", axis=1, tiled=True),
            lax.all_gather(rounded, "row", axis=1, tiled=True),
            rows_feat,
            rows_norm,
        )
        product = lax.psum_scatter(partial_value, "slab", scatter_dimension=1, tiled=True)
        image = product + noise_var[None, :] * direction
        curvature = global_dot(direction, image)
        step_size = res_norm / curvature
        solution = solution + step_size[:, None] * direction
        residual = residual - step_size[:, None] * image
        if iteration + 1 < ITERS:
            new_norm = global_dot(residual, residual)
            direction = residual + (new_norm / res_norm)[:, None] * direction
            res_norm = new_norm
    return (solution, residual)


MESH = pl.DeviceIdType.MESH
NT = (((1,), (1,)), ((), ()))
HALF = 64


def dot_nt(left, right, precision=None):
    return lax.dot_general(left, right, NT, precision=precision, preferred_element_type=jnp.float32)


def lane_mask(rows):
    return lax.broadcasted_iota(jnp.int32, (rows, 128), 1) < HALF


def swap(value):
    return pltpu.roll(value, HALF, 1)


def fold(wide, odd):
    half = wide.shape[0] // 2
    top, bottom = wide[:half], wide[half:]
    if odd:
        return jnp.where(lane_mask(half), swap(top), bottom)
    return jnp.where(lane_mask(half), top, swap(bottom))


def unfold_pair(first, second):
    mask = lane_mask(first.shape[0])
    top = jnp.where(mask, first, swap(second))
    bottom = jnp.where(mask, swap(first), second)
    return jnp.concatenate([top, bottom], axis=0)


def unfold_all(blocks):
    pairs = [unfold_pair(blocks[k], blocks[k + 1]) for k in range(0, len(blocks), 2)]
    return jnp.concatenate(pairs, axis=1)


def split_rows(folded):
    mask = lane_mask(folded.shape[0])
    zero = jnp.zeros_like(folded)
    return jnp.concatenate([jnp.where(mask, folded, zero), jnp.where(mask, zero, folded)], axis=0)


def solve_kernel(
    n_row, n_slab,
    base_hbm, sid_hbm, eid_hbm, station_hbm, epoch_hbm, noise_hbm, right_hbm,
    both_out,
    base_v, sid_v, eid_v, station_v, epoch_v, noise_v, right_v,
    col_v, row_v, kernel_v, near_v, near_in, far_v, far_in, part2_v, sum2_v, mom_v, mom_in,
    load_sem, s_g1, r_g1, s_g1r, r_g1r, s_g2, r_g2, s_g2r, r_g2r, s_rs2, r_rs2, s_ar, r_ar,
):
    row, slab = lax.axis_index("row"), lax.axis_index("slab")
    feat, samples = base_hbm.shape
    vecs = right_hbm.shape[0]
    n_dev = n_row * n_slab

    def row_peer(k):
        return (lax.rem(row + k, n_row), slab)

    def slab_peer(k):
        return (row, lax.rem(slab + k, n_slab))

    def remote(src, dst, send, recv, peer):
        copy = pltpu.make_async_remote_copy(
            src_ref=src, dst_ref=dst, send_sem=send, recv_sem=recv, device_id=peer, device_id_type=MESH
        )
        copy.start()
        return copy

    barrier = pltpu.get_barrier_semaphore()
    for k in range(1, n_row):
        pl.semaphore_signal(barrier, inc=1, device_id=row_peer(k), device_id_type=MESH)
    for k in range(1, n_slab):
        pl.semaphore_signal(barrier, inc=1, device_id=slab_peer(k), device_id_type=MESH)

    loads = []
    for k, (src, dst) in enumerate((
        (sid_hbm, sid_v), (eid_hbm, eid_v), (station_hbm, station_v), (epoch_hbm, epoch_v),
        (base_hbm, base_v), (right_hbm, right_v), (noise_hbm, noise_v),
    )):
        copy = pltpu.make_async_copy(src, dst, load_sem.at[k])
        copy.start()
        loads.append(copy)
    for copy in loads:
        copy.wait()

    def gather(table, ids):
        positions = lax.broadcasted_iota(jnp.int32, (table.shape[1], samples), 0)
        one_hot = jnp.where(positions == ids, 1.0, 0.0).astype(jnp.bfloat16)
        return jnp.dot(table, one_hot, preferred_element_type=jnp.float32)

    right = right_v[...]
    own = (
        base_v[...].astype(jnp.float32)
        + gather(station_v[...], sid_v[...])
        + gather(epoch_v[...], eid_v[...])
    ).astype(jnp.bfloat16).astype(jnp.float32)
    norm = -0.5 * jnp.sum(own * own, axis=0, keepdims=True)
    high = norm.astype(jnp.bfloat16).astype(jnp.float32)
    middle = (norm - high).astype(jnp.bfloat16).astype(jnp.float32)
    low = norm - high - middle
    at = lax.broadcasted_iota(jnp.int32, (8, samples), 0)
    one, nil = jnp.ones((8, samples), jnp.float32), jnp.zeros((8, samples), jnp.float32)
    col_norm = jnp.where(at == 0, high, jnp.where(at == 1, middle, jnp.where(at == 2, low, jnp.where(at < 6, one, nil))))
    row_norm = jnp.where(at < 3, one, jnp.where(at == 3, high, jnp.where(at == 4, middle, jnp.where(at == 5, low, nil))))
    rest = jnp.zeros((128 - feat - vecs - 8, samples), jnp.float32)
    stacked = jnp.concatenate(
        [own, right, col_norm, rest, own, jnp.zeros((vecs, samples), jnp.float32), row_norm, rest], axis=0
    ).astype(jnp.bfloat16)
    eye_r = lax.broadcasted_iota(jnp.int32, (samples, samples), 0)
    eye_c = lax.broadcasted_iota(jnp.int32, (samples, samples), 1)
    eye = jnp.where(eye_r == eye_c, 1.0, 0.0).astype(jnp.bfloat16)
    packs = dot_nt(eye, stacked).astype(jnp.bfloat16)
    col_v[0] = packs[:, :128]
    row_v[0] = packs[:, 128:]

    pl.semaphore_wait(barrier, n_row + n_slab - 2)
    g1 = [remote(col_v.at[0], col_v.at[k], s_g1.at[k], r_g1.at[k], row_peer(k)) for k in range(1, n_row)]
    g1 += [remote(row_v.at[0], row_v.at[k], s_g1r.at[k], r_g1r.at[k], slab_peer(k)) for k in range(1, n_slab)]

    half = vecs // 2
    right_f = jnp.concatenate([right[:half], right[half:]], axis=1)
    noise_f = jnp.concatenate([noise_v[...], noise_v[...]], axis=1)
    pick_r = lax.broadcasted_iota(jnp.int32, (vecs, 128), 0)
    pick_c = lax.broadcasted_iota(jnp.int32, (vecs, 128), 1)
    pick = jnp.where(pick_c == pick_r + feat, 1.0, 0.0).astype(jnp.bfloat16)

    for copy in g1:
        copy.wait_recv()

    cols = col_v[...].reshape(n_row * samples, 128)
    rows = row_v[...].reshape(n_slab * samples, 128)
    logits = dot_nt(cols, rows)
    directions = dot_nt(pick, cols).astype(jnp.bfloat16)
    kernel_v[...] = jnp.exp(jnp.minimum(logits, 0.0)).astype(jnp.bfloat16)
    tile = kernel_v[...]
    part = jnp.dot(directions, tile, preferred_element_type=jnp.float32)

    def reduce_start(part, out_v, in_v, send, recv):
        copies = []
        for k in range(n_slab - 1, -1, -1):
            start = 128 * (k // 2)
            out_v[k] = fold(part[:, start:start + 128], k % 2)
            if k:
                copies.append(remote(out_v.at[k], in_v.at[k], send.at[k], recv.at[k], slab_peer(n_slab - k)))
        return copies

    def reduce_end(copies, out_v, in_v):
        for copy in copies:
            copy.wait_recv()
        total = out_v[0]
        for k in range(1, n_slab):
            total = total + in_v[k]
        return total

    for k in range(n_slab):
        start = 128 * (k // 2)
        piece = fold(part[:, start:start + 128], k % 2)
        if k == 0:
            piece = piece + noise_f * right_f
        near_v[k] = piece
        far_v[k] = piece.astype(jnp.bfloat16)
    g2 = []
    for j in range(1, n_row):
        for k in range(n_slab):
            peer = (lax.rem(row + j, n_row), lax.rem(slab + n_slab - k, n_slab))
            g2.append(remote(far_v.at[k], far_in.at[j, k], s_g2.at[j, k], r_g2.at[j, k], peer))
    near = [remote(near_v, near_in.at[k], s_g2r.at[k], r_g2r.at[k], slab_peer(k)) for k in range(1, n_slab)]
    for copy in near:
        copy.wait_recv()

    def row_image(k):
        total = near_v[k]
        for m in range(1, n_slab):
            total = total + near_in[m, (k - m) % n_slab]
        return total

    row_images = [row_image(k) for k in range(n_slab)]
    image = row_images[0]

    def col_image(j):
        total = far_in[j, 0].astype(jnp.float32)
        for k in range(1, n_slab):
            total = total + far_in[j, k].astype(jnp.float32)
        return total

    early = jnp.concatenate(
        [split_rows(right_f * right_f), split_rows(right_f * image), split_rows(image * image),
         split_rows(noise_f * image * image)], axis=0
    )
    moments = dot_nt(jnp.ones((8, 128), jnp.float32), early, lax.Precision.HIGHEST)

    for copy in g2:
        copy.wait_recv()
    images = unfold_all([image] + [col_image(j) for j in range(1, n_row)]).astype(jnp.bfloat16)
    part = jnp.dot(images, tile, preferred_element_type=jnp.float32)
    rs2 = reduce_start(part, part2_v, sum2_v, s_rs2, r_rs2)
    own_rows = unfold_all(row_images)
    late = jnp.concatenate([jnp.zeros((3 * vecs, part.shape[1]), jnp.float32), own_rows * part], axis=0)
    ones = jnp.ones((8, part.shape[1]), jnp.bfloat16)
    late_high = late.astype(jnp.bfloat16)
    late_low = (late - late_high.astype(jnp.float32)).astype(jnp.bfloat16)
    moments = moments + (dot_nt(ones, late_high) + dot_nt(ones, late_low))
    mom_v[...] = moments[:1]

    me = row * n_slab + slab
    ar = []
    for k in range(1, n_dev):
        other = lax.rem(me + k, n_dev)
        peer = (other // n_slab, lax.rem(other, n_slab))
        ar.append(remote(mom_v, mom_in.at[k], s_ar.at[k], r_ar.at[k], peer))
    second = reduce_end(rs2, part2_v, sum2_v) + noise_f * image
    mask = lane_mask(half)
    image_n = jnp.concatenate([image, swap(image)], axis=0)[:, :samples]
    second_n = jnp.concatenate([second, swap(second)], axis=0)[:, :samples]

    for copy in ar:
        copy.wait_recv()
    total = mom_v[...]
    for k in range(1, n_dev):
        total = total + mom_in[k]
    total = jnp.broadcast_to(total, (8, 128))
    bb = total
    bq, qq, qs = (pltpu.roll(total, 128 - vecs * k, 1) for k in (1, 2, 3))
    alpha = bb / bq
    fresh = bb - 2.0 * alpha * bq + alpha * alpha * qq
    grow = 1.0 + fresh / bb
    curvature = grow * grow * bq - 2.0 * alpha * grow * qq + alpha * alpha * qs
    step = fresh / curvature
    first_c = alpha + step * grow
    second_c = step * alpha

    def column(coefficients):
        spread = jnp.where(pick_r == pick_c, coefficients[:1], 0.0)
        return jnp.sum(spread, axis=1, keepdims=True)

    first_c, second_c = column(first_c), column(second_c)
    both_out[0] = first_c * right - second_c * image_n
    both_out[1] = right - first_c * image_n + second_c * second_n

    for copy in g1 + near + g2 + rs2 + ar:
        copy.wait_send()


def per_device_kernel(
    n_row, n_slab, base_features, station_ids, epoch_ids, station_table, epoch_table, noise_var, right_side
):
    feat, samples = base_features.shape
    vecs = right_side.shape[0]
    n_dev = n_row * n_slab
    bf16, f32 = jnp.bfloat16, jnp.float32
    dma = pltpu.SemaphoreType.DMA
    half = vecs // 2
    operands = (
        base_features, station_ids.reshape(1, samples), epoch_ids.reshape(1, samples),
        station_table, epoch_table, noise_var.reshape(1, samples), right_side,
    )
    shape = jax.ShapeDtypeStruct((2, vecs, samples), f32)
    both = pl.pallas_call(
        functools.partial(solve_kernel, n_row, n_slab),
        out_shape=shape,
        in_specs=[pl.BlockSpec(memory_space=pl.ANY)] * 7,
        out_specs=pl.BlockSpec(memory_space=pltpu.VMEM),
        scratch_shapes=[pltpu.VMEM(x.shape, x.dtype) for x in operands] + [
            pltpu.VMEM((n_row, samples, 128), bf16),
            pltpu.VMEM((n_slab, samples, 128), bf16),
            pltpu.VMEM((n_row * samples, n_slab * samples), bf16),
            pltpu.VMEM((n_slab, half, 128), f32),
            pltpu.VMEM((n_slab, n_slab, half, 128), f32),
            pltpu.VMEM((n_slab, half, 128), bf16),
            pltpu.VMEM((n_row, n_slab, half, 128), bf16),
            pltpu.VMEM((n_slab, half, 128), f32),
            pltpu.VMEM((n_slab, half, 128), f32),
            pltpu.VMEM((1, 128), f32),
            pltpu.VMEM((n_dev, 1, 128), f32),
            dma((7,)),
            dma((n_row,)), dma((n_row,)), dma((n_slab,)), dma((n_slab,)),
            dma((n_row, n_slab)), dma((n_row, n_slab)), dma((n_slab,)), dma((n_slab,)),
            dma((n_slab,)), dma((n_slab,)),
            dma((n_dev,)), dma((n_dev,)),
        ],
        compiler_params=pltpu.CompilerParams(
            collective_id=0, has_side_effects=True, vmem_limit_bytes=60 * 1024 * 1024
        ),
    )(*operands)
    return both[0], both[1]


def solution(mesh):
    in_specs = (
        P(None, ("row", "slab")),
        P(("row", "slab")),
        P(("row", "slab")),
        P(),
        P(),
        P(("row", "slab")),
        P(None, ("row", "slab")),
    )
    out_specs = (P(None, ("row", "slab")), P(None, ("row", "slab")))
    n_row, n_slab = mesh.shape["row"], mesh.shape["slab"]
    body = per_device
    if n_row * n_slab <= 64:
        body = functools.partial(per_device_kernel, n_row, n_slab)
    return jax.shard_map(
        body, mesh=mesh, in_specs=in_specs, out_specs=out_specs, check_vma=False
    )
```

```python
import functools

import jax
import jax.numpy as jnp
from jax import lax
from jax.experimental import pallas as pl
from jax.experimental.pallas import tpu as pltpu
from jax.sharding import PartitionSpec as P

ITERS = 2


def lookup(table, indices):
    positions = lax.broadcasted_iota(jnp.int32, (table.shape[1], indices.shape[0]), 0)
    one_hot = (positions == indices[None, :]).astype(jnp.bfloat16)
    return jnp.dot(table, one_hot, preferred_element_type=jnp.float32)


def column_norms(piece):
    wide_piece = piece.astype(jnp.float32)
    return jnp.sum(wide_piece * wide_piece, axis=0)


def tile_term(col_feat, col_dir, rows_feat, rows_norm):
    cross_term = lax.dot_general(
        col_feat, rows_feat, (((0,), (0,)), ((), ())), preferred_element_type=jnp.float32
    )
    col_norm = column_norms(col_feat)
    distance = jnp.maximum(col_norm[:, None] + rows_norm[None, :] - 2.0 * cross_term, 0.0)
    kernel_tile = jnp.exp(-0.5 * distance).astype(jnp.bfloat16)
    return jnp.dot(col_dir, kernel_tile, preferred_element_type=jnp.float32)


def global_dot(left, right):
    return lax.psum(jnp.sum(left * right, axis=1), ("row", "slab"))


def per_device(
    base_features, station_ids, epoch_ids, station_table, epoch_table, noise_var, right_side
):
    own_feat = (
        base_features.astype(jnp.float32)
        + lookup(station_table, station_ids)
        + lookup(epoch_table, epoch_ids)
    ).astype(jnp.bfloat16)
    rows_feat = lax.all_gather(own_feat, "slab", axis=1, tiled=True)
    rows_norm = column_norms(rows_feat)
    solution = jnp.zeros_like(right_side)
    residual = right_side
    direction = right_side
    res_norm = global_dot(residual, residual)
    for iteration in range(ITERS):
        rounded = direction.astype(jnp.bfloat16)
        partial_value = tile_term(
            lax.all_gather(own_feat, "row", axis=1, tiled=True),
            lax.all_gather(rounded, "row", axis=1, tiled=True),
            rows_feat,
            rows_norm,
        )
        product = lax.psum_scatter(partial_value, "slab", scatter_dimension=1, tiled=True)
        image = product + noise_var[None, :] * direction
        curvature = global_dot(direction, image)
        step_size = res_norm / curvature
        solution = solution + step_size[:, None] * direction
        residual = residual - step_size[:, None] * image
        if iteration + 1 < ITERS:
            new_norm = global_dot(residual, residual)
            direction = residual + (new_norm / res_norm)[:, None] * direction
            res_norm = new_norm
    return (solution, residual)


MESH = pl.DeviceIdType.MESH
NT = (((1,), (1,)), ((), ()))
HALF = 64


def dot_nt(left, right, precision=None):
    return lax.dot_general(left, right, NT, precision=precision, preferred_element_type=jnp.float32)


def lane_mask(rows):
    return lax.broadcasted_iota(jnp.int32, (rows, 128), 1) < HALF


def swap(value):
    return pltpu.roll(value, HALF, 1)


def fold(wide, odd):
    half = wide.shape[0] // 2
    top, bottom = wide[:half], wide[half:]
    if odd:
        return jnp.where(lane_mask(half), swap(top), bottom)
    return jnp.where(lane_mask(half), top, swap(bottom))


def unfold_pair(first, second):
    mask = lane_mask(first.shape[0])
    top = jnp.where(mask, first, swap(second))
    bottom = jnp.where(mask, swap(first), second)
    return jnp.concatenate([top, bottom], axis=0)


def unfold_all(blocks):
    pairs = [unfold_pair(blocks[k], blocks[k + 1]) for k in range(0, len(blocks), 2)]
    return jnp.concatenate(pairs, axis=1)


def split_rows(folded):
    mask = lane_mask(folded.shape[0])
    zero = jnp.zeros_like(folded)
    return jnp.concatenate([jnp.where(mask, folded, zero), jnp.where(mask, zero, folded)], axis=0)


def solve_kernel(
    n_row, n_slab,
    base_hbm, sid_hbm, eid_hbm, station_hbm, epoch_hbm, noise_hbm, right_hbm,
    both_out,
    base_v, sid_v, eid_v, station_v, epoch_v, noise_v, right_v,
    col_v, row_v, kernel_v, near_v, near_in, far_v, far_in, part2_v, sum2_v, mom_v, mom_in,
    load_sem, s_g1, r_g1, s_g1r, r_g1r, s_g2, r_g2, s_g2r, r_g2r, s_rs2, r_rs2, s_ar, r_ar,
):
    row, slab = lax.axis_index("row"), lax.axis_index("slab")
    feat, samples = base_hbm.shape
    vecs = right_hbm.shape[0]
    n_dev = n_row * n_slab

    def row_peer(k):
        return (lax.rem(row + k, n_row), slab)

    def slab_peer(k):
        return (row, lax.rem(slab + k, n_slab))

    def remote(src, dst, send, recv, peer):
        copy = pltpu.make_async_remote_copy(
            src_ref=src, dst_ref=dst, send_sem=send, recv_sem=recv, device_id=peer, device_id_type=MESH
        )
        copy.start()
        return copy

    barrier = pltpu.get_barrier_semaphore()
    for k in range(1, n_row):
        pl.semaphore_signal(barrier, inc=1, device_id=row_peer(k), device_id_type=MESH)
    for k in range(1, n_slab):
        pl.semaphore_signal(barrier, inc=1, device_id=slab_peer(k), device_id_type=MESH)

    loads = []
    for k, (src, dst) in enumerate((
        (sid_hbm, sid_v), (eid_hbm, eid_v), (station_hbm, station_v), (epoch_hbm, epoch_v),
        (base_hbm, base_v), (right_hbm, right_v), (noise_hbm, noise_v),
    )):
        copy = pltpu.make_async_copy(src, dst, load_sem.at[k])
        copy.start()
        loads.append(copy)
    for copy in loads:
        copy.wait()

    def gather(table, ids):
        positions = lax.broadcasted_iota(jnp.int32, (table.shape[1], samples), 0)
        one_hot = jnp.where(positions == ids, 1.0, 0.0).astype(jnp.bfloat16)
        return jnp.dot(table, one_hot, preferred_element_type=jnp.float32)

    right = right_v[...]
    own = (
        base_v[...].astype(jnp.float32)
        + gather(station_v[...], sid_v[...])
        + gather(epoch_v[...], eid_v[...])
    ).astype(jnp.bfloat16).astype(jnp.float32)
    norm = -0.5 * jnp.sum(own * own, axis=0, keepdims=True)
    high = norm.astype(jnp.bfloat16).astype(jnp.float32)
    middle = (norm - high).astype(jnp.bfloat16).astype(jnp.float32)
    low = norm - high - middle
    at = lax.broadcasted_iota(jnp.int32, (8, samples), 0)
    one, nil = jnp.ones((8, samples), jnp.float32), jnp.zeros((8, samples), jnp.float32)
    col_norm = jnp.where(at == 0, high, jnp.where(at == 1, middle, jnp.where(at == 2, low, jnp.where(at < 6, one, nil))))
    row_norm = jnp.where(at < 3, one, jnp.where(at == 3, high, jnp.where(at == 4, middle, jnp.where(at == 5, low, nil))))
    rest = jnp.zeros((128 - feat - vecs - 8, samples), jnp.float32)
    stacked = jnp.concatenate(
        [own, right, col_norm, rest, own, jnp.zeros((vecs, samples), jnp.float32), row_norm, rest], axis=0
    ).astype(jnp.bfloat16)
    eye_r = lax.broadcasted_iota(jnp.int32, (samples, samples), 0)
    eye_c = lax.broadcasted_iota(jnp.int32, (samples, samples), 1)
    eye = jnp.where(eye_r == eye_c, 1.0, 0.0).astype(jnp.bfloat16)
    packs = dot_nt(eye, stacked).astype(jnp.bfloat16)
    col_v[0] = packs[:, :128]
    row_v[0] = packs[:, 128:]

    pl.semaphore_wait(barrier, n_row + n_slab - 2)
    g1 = [remote(col_v.at[0], col_v.at[k], s_g1.at[k], r_g1.at[k], row_peer(k)) for k in sorted(range(1, n_row), key=lambda k: -abs(k - n_row // 2))]
    g1 += [remote(row_v.at[0], row_v.at[k], s_g1r.at[k], r_g1r.at[k], slab_peer(k)) for k in range(1, n_slab)]

    half = vecs // 2
    right_f = jnp.concatenate([right[:half], right[half:]], axis=1)
    noise_f = jnp.concatenate([noise_v[...], noise_v[...]], axis=1)
    pick_r = lax.broadcasted_iota(jnp.int32, (vecs, 128), 0)
    pick_c = lax.broadcasted_iota(jnp.int32, (vecs, 128), 1)
    pick = jnp.where(pick_c == pick_r + feat, 1.0, 0.0).astype(jnp.bfloat16)

    for copy in g1:
        copy.wait_recv()

    cols = col_v[...].reshape(n_row * samples, 128)
    rows = row_v[...].reshape(n_slab * samples, 128)
    logits = dot_nt(cols, rows)
    directions = dot_nt(pick, cols).astype(jnp.bfloat16)
    kernel_v[...] = jnp.exp(jnp.minimum(logits, 0.0)).astype(jnp.bfloat16)
    tile = kernel_v[...]
    part = jnp.dot(directions, tile, preferred_element_type=jnp.float32)

    def reduce_start(part, out_v, in_v, send, recv):
        copies = []
        for k in range(n_slab - 1, -1, -1):
            start = 128 * (k // 2)
            out_v[k] = fold(part[:, start:start + 128], k % 2)
            if k:
                copies.append(remote(out_v.at[k], in_v.at[k], send.at[k], recv.at[k], slab_peer(n_slab - k)))
        return copies

    def reduce_end(copies, out_v, in_v):
        for copy in copies:
            copy.wait_recv()
        total = out_v[0]
        for k in range(1, n_slab):
            total = total + in_v[k]
        return total

    for k in range(n_slab):
        start = 128 * (k // 2)
        piece = fold(part[:, start:start + 128], k % 2)
        if k == 0:
            piece = piece + noise_f * right_f
        near_v[k] = piece
        far_v[k] = piece.astype(jnp.bfloat16)
    g2 = []
    for k in range(n_slab):
        for j in sorted(range(1, n_row), key=lambda j: -abs(j - n_row // 2)):
            peer = (lax.rem(row + j, n_row), lax.rem(slab + n_slab - k, n_slab))
            g2.append(remote(far_v.at[k], far_in.at[j, k], s_g2.at[j, k], r_g2.at[j, k], peer))
    near = [remote(near_v, near_in.at[k], s_g2r.at[k], r_g2r.at[k], slab_peer(k)) for k in range(1, n_slab)]
    for copy in near:
        copy.wait_recv()

    def row_image(k):
        total = near_v[k]
        for m in range(1, n_slab):
            total = total + near_in[m, (k - m) % n_slab]
        return total

    row_images = [row_image(k) for k in range(n_slab)]
    image = row_images[0]

    def col_image(j):
        total = far_in[j, 0].astype(jnp.float32)
        for k in range(1, n_slab):
            total = total + far_in[j, k].astype(jnp.float32)
        return total

    early = jnp.concatenate(
        [split_rows(right_f * right_f), split_rows(right_f * image), split_rows(image * image),
         split_rows(noise_f * image * image)], axis=0
    )
    moments = dot_nt(jnp.ones((8, 128), jnp.float32), early, lax.Precision.HIGHEST)

    for copy in g2:
        copy.wait_recv()
    images = unfold_all([image] + [col_image(j) for j in range(1, n_row)]).astype(jnp.bfloat16)
    part = jnp.dot(images, tile, preferred_element_type=jnp.float32)
    rs2 = reduce_start(part, part2_v, sum2_v, s_rs2, r_rs2)
    own_rows = unfold_all(row_images)
    late = jnp.concatenate([jnp.zeros((3 * vecs, part.shape[1]), jnp.float32), own_rows * part], axis=0)
    ones = jnp.ones((8, part.shape[1]), jnp.bfloat16)
    late_high = late.astype(jnp.bfloat16)
    late_low = (late - late_high.astype(jnp.float32)).astype(jnp.bfloat16)
    moments = moments + (dot_nt(ones, late_high) + dot_nt(ones, late_low))
    mom_v[...] = moments[:1]

    me = row * n_slab + slab
    ar = []
    for k in range(1, n_dev):
        other = lax.rem(me + k, n_dev)
        peer = (other // n_slab, lax.rem(other, n_slab))
        ar.append(remote(mom_v, mom_in.at[k], s_ar.at[k], r_ar.at[k], peer))
    second = reduce_end(rs2, part2_v, sum2_v) + noise_f * image
    mask = lane_mask(half)
    image_n = jnp.concatenate([image, swap(image)], axis=0)[:, :samples]
    second_n = jnp.concatenate([second, swap(second)], axis=0)[:, :samples]

    for copy in ar:
        copy.wait_recv()
    total = mom_v[...]
    for k in range(1, n_dev):
        total = total + mom_in[k]
    total = jnp.broadcast_to(total, (8, 128))
    bb = total
    bq, qq, qs = (pltpu.roll(total, 128 - vecs * k, 1) for k in (1, 2, 3))
    alpha = bb / bq
    fresh = bb - 2.0 * alpha * bq + alpha * alpha * qq
    grow = 1.0 + fresh / bb
    curvature = grow * grow * bq - 2.0 * alpha * grow * qq + alpha * alpha * qs
    step = fresh / curvature
    first_c = alpha + step * grow
    second_c = step * alpha

    def column(coefficients):
        spread = jnp.where(pick_r == pick_c, coefficients[:1], 0.0)
        return jnp.sum(spread, axis=1, keepdims=True)

    first_c, second_c = column(first_c), column(second_c)
    both_out[0] = first_c * right - second_c * image_n
    both_out[1] = right - first_c * image_n + second_c * second_n

    for copy in g1 + near + g2 + rs2 + ar:
        copy.wait_send()


def per_device_kernel(
    n_row, n_slab, base_features, station_ids, epoch_ids, station_table, epoch_table, noise_var, right_side
):
    feat, samples = base_features.shape
    vecs = right_side.shape[0]
    n_dev = n_row * n_slab
    bf16, f32 = jnp.bfloat16, jnp.float32
    dma = pltpu.SemaphoreType.DMA
    half = vecs // 2
    operands = (
        base_features, station_ids.reshape(1, samples), epoch_ids.reshape(1, samples),
        station_table, epoch_table, noise_var.reshape(1, samples), right_side,
    )
    shape = jax.ShapeDtypeStruct((2, vecs, samples), f32)
    both = pl.pallas_call(
        functools.partial(solve_kernel, n_row, n_slab),
        out_shape=shape,
        in_specs=[pl.BlockSpec(memory_space=pl.ANY)] * 7,
        out_specs=pl.BlockSpec(memory_space=pltpu.VMEM),
        scratch_shapes=[pltpu.VMEM(x.shape, x.dtype) for x in operands] + [
            pltpu.VMEM((n_row, samples, 128), bf16),
            pltpu.VMEM((n_slab, samples, 128), bf16),
            pltpu.VMEM((n_row * samples, n_slab * samples), bf16),
            pltpu.VMEM((n_slab, half, 128), f32),
            pltpu.VMEM((n_slab, n_slab, half, 128), f32),
            pltpu.VMEM((n_slab, half, 128), bf16),
            pltpu.VMEM((n_row, n_slab, half, 128), bf16),
            pltpu.VMEM((n_slab, half, 128), f32),
            pltpu.VMEM((n_slab, half, 128), f32),
            pltpu.VMEM((1, 128), f32),
            pltpu.VMEM((n_dev, 1, 128), f32),
            dma((7,)),
            dma((n_row,)), dma((n_row,)), dma((n_slab,)), dma((n_slab,)),
            dma((n_row, n_slab)), dma((n_row, n_slab)), dma((n_slab,)), dma((n_slab,)),
            dma((n_slab,)), dma((n_slab,)),
            dma((n_dev,)), dma((n_dev,)),
        ],
        compiler_params=pltpu.CompilerParams(
            collective_id=0, has_side_effects=True, vmem_limit_bytes=60 * 1024 * 1024
        ),
    )(*operands)
    return both[0], both[1]


def solution(mesh):
    in_specs = (
        P(None, ("row", "slab")),
        P(("row", "slab")),
        P(("row", "slab")),
        P(),
        P(),
        P(("row", "slab")),
        P(None, ("row", "slab")),
    )
    out_specs = (P(None, ("row", "slab")), P(None, ("row", "slab")))
    n_row, n_slab = mesh.shape["row"], mesh.shape["slab"]
    body = per_device
    if n_row * n_slab <= 64:
        body = functools.partial(per_device_kernel, n_row, n_slab)
    return jax.shard_map(
        body, mesh=mesh, in_specs=in_specs, out_specs=out_specs, check_vma=False
    )
```
